32 devices in a mesh: section: 4 (over y, core), phase: 2 (over x), tp: 4 (over z).
Axes of the slice: x: 2, y: 2, z: 4, core: 2. Of those that a mesh axis runs over, the one named last changes fastest.
Arguments:
- hidden_act: bfloat16 [1024, 28672], P(('section', 'phase'), 'tp'), may hold values from -6 to 6
- down_weight: bfloat16 [28672, 8192], P('tp', ('phase', 'section')), may hold values from -0.03125 to 0.03125
- residual: bfloat16 [1024, 8192], P('section', 'phase'), may hold values from -6 to 6
- head_weight: float32 [8192], P('phase'), may hold values from -0.011048543 to 0.011048543
- gain: float32 [8192], P('phase'), may hold values from 0.1 to 1.9
- behavior_policy_logprob: float32 [1024], replicated, may hold values from -6 to -0.05
- frozen_policy_logprob: float32 [1024], replicated, may hold values from -6 to -0.05
- old_values: float32 [1024], replicated, may hold values from -5 to 5
- judge_ratings: float32 [16], replicated, may hold values from -8 to 8
- lengths: int32 [16], replicated, may hold values from 1 to 192, 1024 in all
Outputs:
- total_loss: float32 [], replicated
- head_grad: float32 [8192], P('phase')
- down_projection_gradient: float32 [28672, 8192], P('tp', ('phase', 'section'))
- hidden_grad: bfloat16 [1024, 28672], P(('section', 'phase'), 'tp')
The draws below stay inside these ranges and needn't reach their ends.
Inputs may be any that keep to these rules, and one draw needn't show every extreme that they name: The 16 lengths sum to 1024; the longest is exactly 192.
All inputs are finite; a program needn't handle non-finite values.
Results may differ from the reference program's by a relative error of at most 0.0049.
Values may be sent and summed in bfloat16 or wider, within the bound.
A program may use at most 192 MiB of HBM per device.

```python
import math
import jax
import jax.numpy as jnp
import numpy as np
from jax import lax

D = 8192
FF = 28672
TOKENS = 1024
RESP = 16
MOST = 192


def common_signs(key):
    picks = jax.random.randint(jax.random.fold_in(key, 101), (D,), 0, 2)
    return (2 * picks - 1).astype(jnp.float32)


def draw_head_weight(key, part):
    signs = common_signs(key)
    key = jax.random.fold_in(key, 1)
    magnitude = jnp.abs(jax.random.truncated_normal(key, -4.0, 4.0, (D,), jnp.float32))
    return (signs * magnitude * (0.25 / math.sqrt(D))).astype(jnp.float32)


def draw_residual(key, part):
    signs = common_signs(key)
    key = jax.random.fold_in(key, 2)
    noise_key, pull_key, flip_key = jax.random.split(key, 3)
    flips = (2 * jax.random.randint(flip_key, (TOKENS,), 0, 2) - 1).astype(jnp.float32)
    noise = jax.random.truncated_normal(noise_key, -4.5, 4.5, (TOKENS, D), jnp.float32)
    pull = jax.random.uniform(pull_key, (TOKENS,), jnp.float32, 0.25, 0.8)
    return (noise + (pull * flips)[:, None] * signs[None, :]).astype(jnp.bfloat16)


def block_scale(own_key, extent, cuts, low, top_value):
    loudness, own = 1.0, jax.random.fold_in(own_key, 6)
    for dim, shards_of in cuts:
        draws = jnp.exp(jax.random.uniform(jax.random.fold_in(own, dim), (shards_of,), jnp.float32, low / len(cuts), top_value / len(cuts)))
        loudness = loudness * jnp.repeat(draws, extent[dim] // shards_of).reshape([-1 if axis == dim else 1 for axis in range(len(extent))])
    return loudness


def split_up(amount, total, most, slope):
    weights = [(1 << 20) // math.isqrt(standing ** slope) + 1 for standing in range(2, amount + 1)]
    spare, holding = total - most - (amount - 1), [1] * (amount - 1)
    while spare > 0:
        candidates = [i for i in range(amount - 1) if holding[i] < most]
        pool, left = sum([weights[i] for i in candidates]), spare
        for i in candidates:
            addition = min(most - holding[i], max(1, left * weights[i] // pool), spare)
            holding[i] = holding[i] + addition
            spare = spare - addition
    return np.array([most] + holding)


def uneven_parts(rng, number_of, total, limit, lean):
    if number_of == 2:
        one = jax.random.randint(rng, (), max(1, total - limit), min(limit, total - 1) + 1)
        return jnp.stack([one, total - one])
    sizes = jnp.asarray(split_up(number_of, total, limit, lean), jnp.int32)
    couples = (number_of - 1) // 2
    donor, sink = sizes[1:1 + 2 * couples:2], sizes[2:2 + 2 * couples:2]
    margin = jnp.minimum(donor - 1, limit - sink)
    shifted = jax.random.randint(jax.random.fold_in(rng, 1), (couples,), 0, 1 << 20) % (margin + 1)
    sizes = sizes.at[1:1 + 2 * couples:2].set(donor - shifted).at[2:2 + 2 * couples:2].set(sink + shifted)
    return sizes[jax.random.permutation(jax.random.fold_in(rng, 2), number_of)]


def centred(key, shape, scale, most, cuts=(), kind=jnp.bfloat16):
    array = scale * jax.random.normal(key, shape, jnp.float32)
    if cuts:
        array = array * block_scale(key, shape, cuts, -0.22, 0.18)
    return jnp.clip(array, -most, most).astype(kind)


def setup_inputs(seed: int = 0) -> dict:
    arg_keys = jax.random.split(jax.random.key(seed), 11)
    return {
        "hidden_act": centred(arg_keys[0], (TOKENS, FF), 1.0, 6.0, ((0, 8), (1, 4))),
        "down_weight": centred(arg_keys[1], (FF, D), FF ** -0.5, 0.03125, ((0, 4), (1, 8))),
        "residual": draw_residual(jax.random.fold_in(arg_keys[10], 71), 0),
        "head_weight": draw_head_weight(jax.random.fold_in(arg_keys[10], 71), 0),
        "gain": jnp.clip(1.0 + 0.18 * jax.random.normal(arg_keys[4], (D,), jnp.float32), 0.1, 1.9),
        "behavior_policy_logprob": jnp.clip(jax.random.uniform(arg_keys[5], (TOKENS,), jnp.float32, -6.0, -0.05), -6.0, -0.05),
        "frozen_policy_logprob": jnp.clip(jax.random.uniform(arg_keys[6], (TOKENS,), jnp.float32, -6.0, -0.05), -6.0, -0.05),
        "old_values": centred(arg_keys[7], (TOKENS,), 1.0, 5.0, (), jnp.float32),
        "judge_ratings": centred(arg_keys[8], (RESP,), 2.0, 8.0, (), jnp.float32),
        "lengths": uneven_parts(arg_keys[9], RESP, TOKENS, MOST, 2).astype(jnp.int32),
    }


KL_PENALTY_SCALE = 0.1
TRACE_DECAY = 0.95
CLIP_RANGE = 0.2
EPSILON = 1e-05

def shaped_returns(behavior_policy_logprob, frozen_policy_logprob, old_values, judge_ratings, lengths):
    count = behavior_policy_logprob.shape[0]
    position = jnp.arange(count, dtype=jnp.int32)
    ends = jnp.cumsum(lengths).astype(jnp.int32)
    closes_sequence = position[:, None] == ends[None, :] - 1
    final = jnp.any(closes_sequence, axis=1)
    terminal_payoff_extra = lax.optimization_barrier(jnp.sum(jnp.where(closes_sequence, judge_ratings[None, :], jnp.zeros_like(judge_ratings)[None, :]), axis=1))
    per_position_payoff = terminal_payoff_extra - KL_PENALTY_SCALE * (behavior_policy_logprob - frozen_policy_logprob)
    following = jnp.concatenate([old_values[1:], jnp.zeros_like(old_values[:1])])
    following = jnp.where(final, jnp.zeros_like(following), following)
    delta = per_position_payoff + following - old_values
    segment = lax.optimization_barrier(jnp.sum((position[:, None] >= ends[None, :]).astype(jnp.int32), axis=1))
    gap = position[None, :] - position[:, None]
    inside = (segment[:, None] == segment[None, :]) & (gap >= 0)
    powers = jnp.power(jnp.full_like(delta[:1], TRACE_DECAY)[0], jnp.maximum(gap, 0).astype(delta.dtype))
    weights = jnp.where(inside, powers, jnp.zeros_like(powers))
    advantage = jnp.dot(weights, delta, precision=lax.Precision.HIGHEST)
    return advantage + old_values

def reference(hidden_act, down_weight, residual, head_weight, gain, behavior_policy_logprob, frozen_policy_logprob, old_values, judge_ratings, lengths):
    target_returns = shaped_returns(behavior_policy_logprob, frozen_policy_logprob, old_values, judge_ratings, lengths)
    block_out = jnp.dot(hidden_act, down_weight, preferred_element_type=jnp.float32)
    combined = residual.astype(jnp.float32) + block_out
    width = combined.shape[1]
    rinv = lax.rsqrt(lax.optimization_barrier(jnp.mean(combined * combined, axis=1)) + EPSILON)
    normed = combined * rinv[:, None]
    scale = gain * head_weight
    values = jnp.dot(normed, scale, precision=lax.Precision.HIGHEST)
    squash = jnp.tanh((values - old_values) / CLIP_RANGE)
    clipped = old_values + CLIP_RANGE * squash
    first = (values - target_returns) ** 2
    second = (clipped - target_returns) ** 2
    total_loss = 0.25 * jnp.sum(first + second)
    dvalue = 0.5 * (values - target_returns) + 0.5 * (clipped - target_returns) * (1.0 - squash * squash)
    head_grad = gain * lax.optimization_barrier(jnp.sum(normed * dvalue[:, None], axis=0))
    grad_rows = ((dvalue * rinv)[:, None] * (scale[None, :] - normed * (values / width)[:, None])).astype(jnp.bfloat16)
    down_projection_gradient = lax.dot_general(hidden_act, grad_rows, (((0,), (0,)), ((), ())), preferred_element_type=jnp.float32)
    hidden_grad = lax.dot_general(grad_rows, down_weight, (((1,), (1,)), ((), ())), preferred_element_type=jnp.float32).astype(jnp.bfloat16)
    return (total_loss, head_grad, down_projection_gradient, hidden_grad)
```

```python
import jax
import jax.numpy as jnp
from jax import lax
from jax.sharding import PartitionSpec as P

D = 8192

KL_PENALTY_SCALE = 0.1
TRACE_DECAY = 0.95
CLIP_RANGE = 0.2
EPSILON = 1e-05
BF16 = jnp.bfloat16
F32 = jnp.float32


def returns_at(row_pos, behavior, frozen, old_values, judge_ratings, lengths):
    total = behavior.shape[0]
    position = jnp.arange(total, dtype=jnp.int32)
    ends = jnp.cumsum(lengths)
    closes = position[:, None] == ends[None, :] - 1
    final = jnp.any(closes, axis=1)
    extra = jnp.sum(jnp.where(closes, judge_ratings[None, :], 0.0), axis=1)
    payoff = extra - KL_PENALTY_SCALE * (behavior - frozen)
    following = jnp.concatenate([old_values[1:], jnp.zeros_like(old_values[:1])])
    following = jnp.where(final, 0.0, following)
    delta = payoff + following - old_values
    segment = jnp.sum((position[:, None] >= ends[None, :]).astype(jnp.int32), axis=1)
    row_seg = jnp.sum((row_pos[:, None] >= ends[None, :]).astype(jnp.int32), axis=1)
    gap = position[None, :] - row_pos[:, None]
    inside = (row_seg[:, None] == segment[None, :]) & (gap >= 0)
    powers = jnp.power(F32(TRACE_DECAY), jnp.maximum(gap, 0).astype(F32))
    advantage = jnp.sum(jnp.where(inside, powers, 0.0) * delta[None, :], axis=1)
    own_old = jnp.sum(jnp.where(gap == 0, old_values[None, :], 0.0), axis=1)
    return advantage + own_old, own_old


def on_device(mesh_shape, hidden_act, down_weight, residual, head_weight, gain,
              behavior, frozen, old_values, judge_ratings, lengths):
    S, Q, T = mesh_shape["section"], mesh_shape["phase"], mesh_shape["tp"]
    s, p, t = (lax.axis_index(a) for a in ("section", "phase", "tp"))
    rows, FF = hidden_act.shape
    C = down_weight.shape[1]
    K = 2 if rows % (4 * T) == 0 else 1
    piece = rows // (2 * K)
    sub = piece // T
    sizes = {"section": S, "phase": Q, "tp": T}

    def xchg(x, axis, mask):
        return lax.ppermute(x, axis, [(i, i ^ mask) for i in range(sizes[axis])])

    phase_steps = [("phase", 1 << i) for i in range(Q.bit_length() - 1)]
    section_steps = [("section", 1 << i) for i in range(1, S.bit_length() - 1)]
    orders = [phase_steps + section_steps, section_steps + phase_steps]
    held = []
    for steps in orders:
        rs = [0]
        for axis, mask in steps:
            bit = mask * Q if axis == "section" else mask
            rs = rs + [r ^ bit for r in rs]
        held.append(rs)
    nb = len(held[0])
    me = s * Q + p
    own = hidden_act.reshape(K, 2, 1, piece, FF)

    res = residual.reshape(Q, K, 2, T, sub, S, C)
    res = lax.dynamic_index_in_dim(res, t, 3, keepdims=False)
    for i in range(Q.bit_length() - 1):
        pairs = res.reshape((Q >> (i + 1), 2, 1 << i) + res.shape[1:])
        pairs = jnp.where((p >> i) & 1 == 1, pairs[:, ::-1], pairs)
        res = pairs.reshape(res.shape)
    res_by = []
    for m in range(S):
        part = lax.dynamic_index_in_dim(res, s ^ m, 4, keepdims=False)
        res_by.append(part if m == 0 else xchg(part, "section", m))

    pieces = [[None, None] for _ in range(K)]
    token = None
    for k in range(K):
        a, b = own[k, 0], own[k, 1]
        if token is not None:
            a, b, token = lax.optimization_barrier((a, b, token))
        cur = [a, b]
        for j in range(len(orders[0])):
            got = [xchg(cur[h], *orders[h][j]) for h in range(2)]
            cur = [jnp.concatenate([cur[h], got[h]], axis=0) for h in range(2)]
            token = got[0][0, 0, :1]
        here = jnp.stack(cur)
        pieces[k] = [here, xchg(here, "section", 1)]

    def reduce_tp(x):
        n, bit = T, 1
        while n > 1:
            y = x.reshape(x.shape[0], n // 2, 2, sub, C)
            up = (t & bit) != 0
            send = jnp.where(up, y[:, :, 0], y[:, :, 1]).astype(BF16)
            keep = jnp.where(up, y[:, :, 1], y[:, :, 0])
            x = keep + xchg(send, "tp", bit).astype(F32)
            n, bit = n // 2, bit * 2
        return x.reshape(-1, sub, C)

    def gather_tp(x):
        x = x[:, None]
        bit = T // 2
        while bit >= 1:
            got = xchg(x, "tp", bit)
            up = (t & bit) != 0
            lo, hi = jnp.where(up, got, x), jnp.where(up, x, got)
            x = jnp.stack([lo, hi], axis=2).reshape(x.shape[0], -1, sub, C)
            bit //= 2
        return x

    scale = lax.dynamic_slice_in_dim(gain * head_weight, s * C, C, 0)
    combined = [[None, None] for _ in range(K)]
    for k in range(K):
        for c in range(2):
            out = jnp.dot(pieces[k][c].reshape(-1, FF), down_weight, preferred_element_type=F32)
            out = reduce_tp(out.reshape(2 * nb, T, sub, C))
            base = []
            for h in range(2):
                for r in held[h]:
                    rr = r ^ (c * Q)
                    base.append(res_by[rr // Q][rr % Q, k, h])
            combined[k][c] = jnp.stack(base).astype(F32) + out

    blocks = S * Q
    rel = jnp.array([[r ^ (c * Q) for r in held[h]] for c in range(2) for h in range(2)], jnp.int32)
    place = (rel ^ me)[..., None] == jnp.arange(blocks, dtype=jnp.int32)
    place = place.reshape(2, 2, nb, blocks)
    loss_sum = F32(0)
    head_sum = jnp.zeros((C,), F32)
    grads = [[None, None] for _ in range(K)]
    for k in range(K):
        x = jnp.stack(combined[k]).reshape(2, 2, nb, sub, C)
        sums = jnp.stack([jnp.sum(x * x, axis=-1), jnp.sum(x * scale, axis=-1)])
        sums = jnp.sum(jnp.where(place[None, ..., None], sums[:, :, :, :, None, :], 0.0), axis=(1, 3))
        square_sum, product_sum = lax.psum(sums, ("section", "phase"))
        row_pos = (
            jnp.arange(blocks, dtype=jnp.int32)[None, :, None] * rows
            + ((k * 2 + jnp.arange(2, dtype=jnp.int32)[:, None, None]) * T + t) * sub
            + jnp.arange(sub, dtype=jnp.int32)[None, None, :]
        )
        target, old = returns_at(row_pos.reshape(-1), behavior, frozen, old_values, judge_ratings, lengths)
        target, old = target.reshape(square_sum.shape), old.reshape(square_sum.shape)
        rinv = lax.rsqrt(square_sum / D + EPSILON)
        values = rinv * product_sum
        squash = jnp.tanh((values - old) / CLIP_RANGE)
        clipped = old + CLIP_RANGE * squash
        loss_sum += 0.25 * jnp.sum((values - target) ** 2 + (clipped - target) ** 2)
        dvalue = 0.5 * (values - target) + 0.5 * (clipped - target) * (1.0 - squash * squash)
        rowwise = jnp.stack([rinv, dvalue, values / D])
        rowwise = jnp.sum(
            jnp.where(place[None, ..., None], rowwise[:, None, :, None], 0.0), axis=4
        )[..., None]
        normed = x * rowwise[0]
        head_sum += jnp.sum(normed * rowwise[1], axis=(0, 1, 2, 3))
        g = (rowwise[1] * rowwise[0] * (scale - normed * rowwise[2])).astype(BF16)
        for c in (1, 0):
            grads[k][c] = gather_tp(g[c].reshape(2 * nb, sub, C)).reshape(-1, C)

    hidden_rows = []
    for k in range(K):
        far, near = (
            lax.dot_general(grads[k][c], down_weight, (((1,), (1,)), ((), ())), preferred_element_type=F32)
            .reshape(2, nb, piece, FF)
            for c in (1, 0)
        )
        total = near + xchg(far.astype(BF16), "section", 1).astype(F32)
        for h in range(2):
            x = total[h]
            for axis, mask in reversed(orders[h]):
                half = x.shape[0] // 2
                x = x[:half] + xchg(x[half:].astype(BF16), axis, mask).astype(F32)
            hidden_rows.append(x.reshape(piece, FF).astype(BF16))
    hidden_grad = jnp.concatenate(hidden_rows, axis=0)

    all_hidden = jnp.concatenate([pieces[k][c].reshape(-1, FF) for k in range(K) for c in range(2)])
    all_grads = jnp.concatenate([grads[k][c] for k in range(K) for c in range(2)])
    down_projection_gradient = lax.dot_general(
        all_hidden, all_grads, (((0,), (0,)), ((), ())), preferred_element_type=F32
    )

    mine = jnp.arange(S) == s
    packed = jnp.concatenate([
        jnp.where(mine[:, None], head_sum[None, :], 0.0).reshape(-1),
        jnp.where(s == 0, loss_sum, 0.0)[None],
    ])
    packed = lax.psum(packed, ("section", "tp"))
    return (packed[-1], gain * packed[:-1], down_projection_gradient, hidden_grad)


def solution(mesh):
    shape = dict(mesh.shape)
    in_specs = (
        P(("section", "phase"), "tp"),
        P("tp", ("phase", "section")),
        P("section", "phase"),
        P("phase"),
        P("phase"),
        P(),
        P(),
        P(),
        P(),
        P(),
    )
    out_specs = (P(), P("phase"), P("tp", ("phase", "section")), P(("section", "phase"), "tp"))

    def run(*args):
        return on_device(shape, *args)

    return jax.shard_map(run, mesh=mesh, in_specs=in_specs, out_specs=out_specs, check_vma=False)
```

```python
import functools

import jax
import jax.numpy as jnp
from jax import lax
from jax.experimental import pallas as pl
from jax.experimental.layout import Layout, with_layout_constraint
from jax.experimental.pallas import tpu as pltpu
from jax.sharding import PartitionSpec as P

D = 8192

KL_PENALTY_SCALE = 0.1
TRACE_DECAY = 0.95
CLIP_RANGE = 0.2
EPSILON = 1e-05
BF16 = jnp.bfloat16
F32 = jnp.float32


def returns_at(row_pos, behavior, frozen, old_values, judge_ratings, lengths):
    total = behavior.shape[0]
    position = jnp.arange(total, dtype=jnp.int32)
    ends = jnp.cumsum(lengths)
    closes = position[:, None] == ends[None, :] - 1
    final = jnp.any(closes, axis=1)
    extra = jnp.sum(jnp.where(closes, judge_ratings[None, :], 0.0), axis=1)
    payoff = extra - KL_PENALTY_SCALE * (behavior - frozen)
    following = jnp.concatenate([old_values[1:], jnp.zeros_like(old_values[:1])])
    following = jnp.where(final, 0.0, following)
    delta = payoff + following - old_values
    segment = jnp.sum((position[:, None] >= ends[None, :]).astype(jnp.int32), axis=1)
    row_seg = jnp.sum((row_pos[:, None] >= ends[None, :]).astype(jnp.int32), axis=1)
    gap = position[None, :] - row_pos[:, None]
    inside = (row_seg[:, None] == segment[None, :]) & (gap >= 0)
    powers = jnp.power(F32(TRACE_DECAY), jnp.maximum(gap, 0).astype(F32))
    advantage = jnp.sum(jnp.where(inside, powers, 0.0) * delta[None, :], axis=1)
    own_old = jnp.sum(jnp.where(gap == 0, old_values[None, :], 0.0), axis=1)
    return advantage + own_old, own_old


def exchange_kernel(axes, sizes, x_ref, out_ref, slots, send_sems, recv_sems):
    n0, n1 = sizes
    n = n0 * n1
    a, b = lax.axis_index(axes[0]), lax.axis_index(axes[1])
    me = a * n1 + b

    def partner(i):
        return {axes[0]: lax.rem(a + i // n1, n0), axes[1]: lax.rem(b + i % n1, n1)}

    barrier = pltpu.get_barrier_semaphore()
    for i in range(1, n):
        pl.semaphore_signal(barrier, inc=1, device_id=partner(i), device_id_type=pl.DeviceIdType.MESH)
    pl.semaphore_wait(barrier, n - 1)
    copies = []
    for i in range(1, n):
        copy = pltpu.make_async_remote_copy(
            src_ref=x_ref, dst_ref=slots.at[me], send_sem=send_sems.at[i], recv_sem=recv_sems.at[i],
            device_id=partner(i), device_id_type=pl.DeviceIdType.MESH,
        )
        copy.start()
        copies.append(copy)
    slots[me] = x_ref[...]
    for copy in copies:
        copy.wait()
    out_ref[...] = slots[...]


def share(x, axes, sizes, collective_id):
    count = x.size
    tiles = -(-count // 1024) * 8
    flat = jnp.pad(x.reshape(-1), (0, tiles * 128 - count)).reshape(tiles, 128)
    n = sizes[0] * sizes[1]
    out = pl.pallas_call(
        functools.partial(exchange_kernel, axes, sizes),
        out_shape=jax.ShapeDtypeStruct((n, tiles, 128), F32),
        in_specs=[pl.BlockSpec(memory_space=pltpu.VMEM)],
        out_specs=pl.BlockSpec(memory_space=pltpu.VMEM),
        scratch_shapes=[
            pltpu.VMEM((n, tiles, 128), F32),
            pltpu.SemaphoreType.DMA((n,)),
            pltpu.SemaphoreType.DMA((n,)),
        ],
        compiler_params=pltpu.CompilerParams(collective_id=collective_id, has_side_effects=True),
    )(flat)
    return out.reshape(n, -1)[:, :count].reshape((n,) + x.shape)


def on_device(mesh_shape, hidden_act, down_weight, residual, head_weight, gain,
              behavior, frozen, old_values, judge_ratings, lengths):
    S, Q, T = mesh_shape["section"], mesh_shape["phase"], mesh_shape["tp"]
    s, p, t = (lax.axis_index(a) for a in ("section", "phase", "tp"))
    rows, FF = hidden_act.shape
    C = down_weight.shape[1]
    K = 2 if rows % (4 * T) == 0 else 1
    piece = rows // (2 * K)
    sub = piece // T
    sizes = {"section": S, "phase": Q, "tp": T}

    def xchg(x, axis, mask):
        return lax.ppermute(x, axis, [(i, i ^ mask) for i in range(sizes[axis])])

    phase_steps = [("phase", 1 << i) for i in range(Q.bit_length() - 1)]
    section_steps = [("section", 1 << i) for i in range(1, S.bit_length() - 1)]
    orders = [phase_steps + section_steps, section_steps + phase_steps]
    held = []
    for steps in orders:
        rs = [0]
        for axis, mask in steps:
            bit = mask * Q if axis == "section" else mask
            rs = rs + [r ^ bit for r in rs]
        held.append(rs)
    nb = len(held[0])
    me = s * Q + p
    own = hidden_act.reshape(K, 2, 1, piece, FF)

    pieces = [[None, None] for _ in range(K)]
    token = None
    for k in range(K):
        a, b = own[k, 0], own[k, 1]
        if token is not None:
            a, b = a + 0 * token, b + 0 * token
        cur = [a, b]
        for j in range(len(orders[0])):
            got = [xchg(cur[h], *orders[h][j]) for h in range(2)]
            cur = [jnp.concatenate([cur[h], got[h]], axis=0) for h in range(2)]
            token = got[0][0, 0, :1]
        here = jnp.stack(cur)
        if k == 0:
            first_token = token
        pieces[k] = [here, xchg(here, "section", 1)]

    res = (residual + 0 * first_token).reshape(Q, K, 2, T, sub, S, C)
    res = lax.dynamic_index_in_dim(res, t, 3, keepdims=False)
    for i in range(Q.bit_length() - 1):
        pairs = res.reshape((Q >> (i + 1), 2, 1 << i) + res.shape[1:])
        pairs = jnp.where((p >> i) & 1 == 1, pairs[:, ::-1], pairs)
        res = pairs.reshape(res.shape)
    res_by = []
    for m in range(S):
        part = lax.dynamic_index_in_dim(res, s ^ m, 4, keepdims=False)
        res_by.append(part if m == 0 else xchg(part, "section", m))

    def reduce_tp(x):
        n, bit = T, 1
        while n > 1:
            y = x.reshape(x.shape[0], n // 2, 2, sub, C)
            up = (t & bit) != 0
            send = jnp.where(up, y[:, :, 0], y[:, :, 1]).astype(BF16)
            keep = jnp.where(up, y[:, :, 1], y[:, :, 0])
            x = keep + xchg(send, "tp", bit).astype(F32)
            n, bit = n // 2, bit * 2
        return x.reshape(-1, sub, C)

    def gather_tp(x):
        x = x[:, None]
        bit = T // 2
        while bit >= 1:
            got = xchg(x, "tp", bit)
            up = (t & bit) != 0
            lo, hi = jnp.where(up, got, x), jnp.where(up, x, got)
            x = jnp.stack([lo, hi], axis=2).reshape(x.shape[0], -1, sub, C)
            bit //= 2
        return x

    scale = lax.dynamic_slice_in_dim(gain * head_weight, s * C, C, 0)
    combined = [None] * K
    for k in range(K):
        outs = [
            jnp.dot(pieces[k][c].reshape(-1, FF), down_weight, preferred_element_type=F32)
            .reshape(2 * nb, T, sub, C)
            for c in range(2)
        ]
        out = reduce_tp(jnp.concatenate(outs))
        base = []
        for c in range(2):
            for h in range(2):
                for r in held[h]:
                    rr = r ^ (c * Q)
                    base.append(res_by[rr // Q][rr % Q, k, h])
        combined[k] = jnp.stack(base).astype(F32) + out

    blocks = S * Q
    rel = jnp.array([[r ^ (c * Q) for r in held[h]] for c in range(2) for h in range(2)], jnp.int32)
    place = (rel ^ me)[..., None] == jnp.arange(blocks, dtype=jnp.int32)
    place = place.reshape(2, 2, nb, blocks)
    loss_sum = F32(0)
    head_sum = jnp.zeros((C,), F32)
    grads = [[None, None] for _ in range(K)]
    for k in range(K):
        x = combined[k].reshape(2, 2, nb, sub, C)
        sums = jnp.stack([jnp.sum(x * x, axis=-1), jnp.sum(x * scale, axis=-1)])
        sums = jnp.sum(jnp.where(place[None, ..., None], sums[:, :, :, :, None, :], 0.0), axis=(1, 3))
        square_sum, product_sum = jnp.sum(share(sums, ("section", "phase"), (S, Q), 0), axis=0)
        row_pos = (
            jnp.arange(blocks, dtype=jnp.int32)[None, :, None] * rows
            + ((k * 2 + jnp.arange(2, dtype=jnp.int32)[:, None, None]) * T + t) * sub
            + jnp.arange(sub, dtype=jnp.int32)[None, None, :]
        )
        target, old = returns_at(row_pos.reshape(-1), behavior, frozen, old_values, judge_ratings, lengths)
        target, old = target.reshape(square_sum.shape), old.reshape(square_sum.shape)
        rinv = lax.rsqrt(square_sum / D + EPSILON)
        values = rinv * product_sum
        squash = jnp.tanh((values - old) / CLIP_RANGE)
        clipped = old + CLIP_RANGE * squash
        loss_sum += 0.25 * jnp.sum((values - target) ** 2 + (clipped - target) ** 2)
        dvalue = 0.5 * (values - target) + 0.5 * (clipped - target) * (1.0 - squash * squash)
        rowwise = jnp.stack([rinv, dvalue, values / D])
        rowwise = jnp.sum(
            jnp.where(place[None, ..., None], rowwise[:, None, :, None], 0.0), axis=4
        )[..., None]
        normed = x * rowwise[0]
        head_sum += jnp.sum(normed * rowwise[1], axis=(0, 1, 2, 3))
        g = (rowwise[1] * rowwise[0] * (scale - normed * rowwise[2])).astype(BF16)
        g = gather_tp(g.reshape(4 * nb, sub, C)).reshape(2, -1, C)
        grads[k] = [g[0], g[1]]

    turned = with_layout_constraint(down_weight.T, Layout((0, 1)))
    hidden_rows = []
    for k in range(K):
        far, near = (
            jnp.dot(grads[k][c], turned, preferred_element_type=F32)
            .reshape(2, nb, piece, FF)
            for c in (1, 0)
        )
        total = near + xchg(far.astype(BF16), "section", 1).astype(F32)
        for h in range(2):
            x = total[h]
            for axis, mask in reversed(orders[h]):
                half = x.shape[0] // 2
                x = x[:half] + xchg(x[half:].astype(BF16), axis, mask).astype(F32)
            hidden_rows.append(x.reshape(piece, FF).astype(BF16))
    hidden_grad = jnp.concatenate(hidden_rows, axis=0)

    all_hidden = jnp.concatenate([pieces[k][c].reshape(-1, FF) for k in range(K) for c in range(2)])
    all_grads = jnp.concatenate([grads[k][c] for k in range(K) for c in range(2)])
    all_grads = all_grads + 0 * total[0, 0, 0, :1].astype(BF16)
    down_projection_gradient = lax.dot_general(
        all_hidden, all_grads, (((0,), (0,)), ((), ())), preferred_element_type=F32
    )

    packed = jnp.concatenate([head_sum, loss_sum[None]])
    packed = share(packed, ("section", "tp"), (S, T), 1).reshape(S, T, -1)
    packed = jnp.sum(packed, axis=1)
    total_loss, head_all = packed[0, -1], packed[:, :-1].reshape(-1)
    return (total_loss, gain * head_all, down_projection_gradient, hidden_grad)


def solution(mesh):
    shape = dict(mesh.shape)
    in_specs = (
        P(("section", "phase"), "tp"),
        P("tp", ("phase", "section")),
        P("section", "phase"),
        P("phase"),
        P("phase"),
        P(),
        P(),
        P(),
        P(),
        P(),
    )
    out_specs = (P(), P("phase"), P("tp", ("phase", "section")), P(("section", "phase"), "tp"))

    def run(*args):
        return on_device(shape, *args)

    return jax.shard_map(run, mesh=mesh, in_specs=in_specs, out_specs=out_specs, check_vma=False)
```

```python
import functools

import jax
import jax.numpy as jnp
from jax import lax
from jax.experimental import pallas as pl
from jax.experimental.layout import Layout, with_layout_constraint
from jax.experimental.pallas import tpu as pltpu
from jax.sharding import PartitionSpec as P

D = 8192

KL_PENALTY_SCALE = 0.1
TRACE_DECAY = 0.95
CLIP_RANGE = 0.2
EPSILON = 1e-05
BF16 = jnp.bfloat16
F32 = jnp.float32


def returns_at(row_pos, behavior, frozen, old_values, judge_ratings, lengths):
    total = behavior.shape[0]
    position = jnp.arange(total, dtype=jnp.int32)
    ends = jnp.cumsum(lengths)
    closes = position[:, None] == ends[None, :] - 1
    final = jnp.any(closes, axis=1)
    extra = jnp.sum(jnp.where(closes, judge_ratings[None, :], 0.0), axis=1)
    payoff = extra - KL_PENALTY_SCALE * (behavior - frozen)
    following = jnp.concatenate([old_values[1:], jnp.zeros_like(old_values[:1])])
    following = jnp.where(final, 0.0, following)
    delta = payoff + following - old_values
    segment = jnp.sum((position[:, None] >= ends[None, :]).astype(jnp.int32), axis=1)
    row_seg = jnp.sum((row_pos[:, None] >= ends[None, :]).astype(jnp.int32), axis=1)
    gap = position[None, :] - row_pos[:, None]
    inside = (row_seg[:, None] == segment[None, :]) & (gap >= 0)
    powers = jnp.power(F32(TRACE_DECAY), jnp.maximum(gap, 0).astype(F32))
    advantage = jnp.sum(jnp.where(inside, powers, 0.0) * delta[None, :], axis=1)
    own_old = jnp.sum(jnp.where(gap == 0, old_values[None, :], 0.0), axis=1)
    return advantage + own_old, own_old


def exchange_kernel(axes, sizes, x_ref, out_ref, slots, send_sems, recv_sems):
    n0, n1 = sizes
    n = n0 * n1
    a, b = lax.axis_index(axes[0]), lax.axis_index(axes[1])
    me = a * n1 + b

    def partner(i):
        return {axes[0]: lax.rem(a + i // n1, n0), axes[1]: lax.rem(b + i % n1, n1)}

    barrier = pltpu.get_barrier_semaphore()
    for i in range(1, n):
        pl.semaphore_signal(barrier, inc=1, device_id=partner(i), device_id_type=pl.DeviceIdType.MESH)
    pl.semaphore_wait(barrier, n - 1)
    copies = []
    for i in range(1, n):
        copy = pltpu.make_async_remote_copy(
            src_ref=x_ref, dst_ref=slots.at[me], send_sem=send_sems.at[i], recv_sem=recv_sems.at[i],
            device_id=partner(i), device_id_type=pl.DeviceIdType.MESH,
        )
        copy.start()
        copies.append(copy)
    slots[me] = x_ref[...]
    for copy in copies:
        copy.wait()
    out_ref[...] = slots[...]


def share(x, axes, sizes, collective_id):
    count = x.size
    tiles = -(-count // 1024) * 8
    flat = jnp.pad(x.reshape(-1), (0, tiles * 128 - count)).reshape(tiles, 128)
    n = sizes[0] * sizes[1]
    out = pl.pallas_call(
        functools.partial(exchange_kernel, axes, sizes),
        out_shape=jax.ShapeDtypeStruct((n, tiles, 128), F32),
        in_specs=[pl.BlockSpec(memory_space=pltpu.VMEM)],
        out_specs=pl.BlockSpec(memory_space=pltpu.VMEM),
        scratch_shapes=[
            pltpu.VMEM((n, tiles, 128), F32),
            pltpu.SemaphoreType.DMA((n,)),
            pltpu.SemaphoreType.DMA((n,)),
        ],
        compiler_params=pltpu.CompilerParams(collective_id=collective_id, has_side_effects=True),
    )(flat)
    return out.reshape(n, -1)[:, :count].reshape((n,) + x.shape)


def on_device(mesh_shape, hidden_act, down_weight, residual, head_weight, gain,
              behavior, frozen, old_values, judge_ratings, lengths):
    S, Q, T = mesh_shape["section"], mesh_shape["phase"], mesh_shape["tp"]
    s, p, t = (lax.axis_index(a) for a in ("section", "phase", "tp"))
    rows, FF = hidden_act.shape
    C = down_weight.shape[1]
    K = 2 if rows % (4 * T) == 0 else 1
    piece = rows // (2 * K)
    sub = piece // T
    sizes = {"section": S, "phase": Q, "tp": T}

    def xchg(x, axis, mask):
        return lax.ppermute(x, axis, [(i, i ^ mask) for i in range(sizes[axis])])

    phase_steps = [("phase", 1 << i) for i in range(Q.bit_length() - 1)]
    section_steps = [("section", 1 << i) for i in range(1, S.bit_length() - 1)]
    orders = [phase_steps + section_steps, section_steps + phase_steps]
    held = []
    for steps in orders:
        rs = [0]
        for axis, mask in steps:
            bit = mask * Q if axis == "section" else mask
            rs = rs + [r ^ bit for r in rs]
        held.append(rs)
    nb = len(held[0])
    me = s * Q + p
    own = hidden_act.reshape(K, 2, 1, piece, FF)

    def after(x, *others):
        for y in others:
            x = x + (0 * y[(0,) * y.ndim]).astype(x.dtype)
        return x

    def residual_parts(token):
        res = after(residual, token).reshape(Q, K, 2, T, sub, S, C)
        res = lax.dynamic_index_in_dim(res, t, 3, keepdims=False)
        for i in range(Q.bit_length() - 1):
            pairs = res.reshape((Q >> (i + 1), 2, 1 << i) + res.shape[1:])
            pairs = jnp.where((p >> i) & 1 == 1, pairs[:, ::-1], pairs)
            res = pairs.reshape(res.shape)
        res_by = []
        for m in range(S):
            part = lax.dynamic_index_in_dim(res, s ^ m, 4, keepdims=False)
            res_by.append(part if m == 0 else xchg(part, "section", m))
        return res_by

    def reduce_tp(x):
        n, bit = T, 1
        while n > 1:
            y = x.reshape(x.shape[0], n // 2, 2, sub, C)
            up = (t & bit) != 0
            send = jnp.where(up, y[:, :, 0], y[:, :, 1]).astype(BF16)
            keep = jnp.where(up, y[:, :, 1], y[:, :, 0])
            x = keep + xchg(send, "tp", bit).astype(F32)
            n, bit = n // 2, bit * 2
        return x.reshape(-1, sub, C)

    def gather_tp(x):
        x = x[:, None]
        bit = T // 2
        while bit >= 1:
            got = xchg(x, "tp", bit)
            up = (t & bit) != 0
            lo, hi = jnp.where(up, got, x), jnp.where(up, x, got)
            x = jnp.stack([lo, hi], axis=2).reshape(x.shape[0], -1, sub, C)
            bit //= 2
        return x

    scale = lax.dynamic_slice_in_dim(gain * head_weight, s * C, C, 0)
    turned = with_layout_constraint(down_weight.T, Layout((0, 1)))
    pieces = [None] * K
    combined = [None] * K
    first, second, third = [], [], []
    for k in range(K):
        cur = [after(own[k, h], *first) for h in range(2)]
        for j in range(len(orders[0])):
            got = [xchg(cur[h], *orders[h][j]) for h in range(2)]
            cur = [jnp.concatenate([cur[h], got[h]], axis=0) for h in range(2)]
            if j == 0:
                cur = [after(x, *second) for x in cur]
        here = after(jnp.stack(cur), *third)
        pieces[k] = [here, xchg(here, "section", 1)]
        if k == 0:
            res_by = residual_parts(got[0])
        outs = [
            jnp.dot(pieces[k][c].reshape(-1, FF), down_weight, preferred_element_type=F32)
            .reshape(2 * nb, T, sub, C)
            for c in range(2)
        ]
        base = []
        for c in range(2):
            for h in range(2):
                for r in held[h]:
                    rr = r ^ (c * Q)
                    base.append(res_by[rr // Q][rr % Q, k, h])
        combined[k] = (jnp.stack(base), outs)
        first, second = [got[0], got[1], jnp.max(turned[:16, :128], axis=0)], [outs[1]]
        if k == 0:
            out = reduce_tp(jnp.concatenate(outs))
            combined[k] = combined[k][0].astype(F32) + out
            third = [combined[k]]

    blocks = S * Q
    rel = jnp.array([[r ^ (c * Q) for r in held[h]] for c in range(2) for h in range(2)], jnp.int32)
    place = (rel ^ me)[..., None] == jnp.arange(blocks, dtype=jnp.int32)
    place = place.reshape(2, 2, nb, blocks)
    loss_sum = F32(0)
    head_sum = jnp.zeros((C,), F32)
    grads = [[None, None] for _ in range(K)]
    for k in range(K):
        if k > 0:
            base, outs = combined[k]
            out = reduce_tp(after(jnp.concatenate(outs), local))
            combined[k] = after(base.astype(F32) + out, grads[k - 1][0])
        x = combined[k].reshape(2, 2, nb, sub, C)
        sums = jnp.stack([jnp.sum(x * x, axis=-1), jnp.sum(x * scale, axis=-1)])
        sums = jnp.sum(jnp.where(place[None, ..., None], sums[:, :, :, :, None, :], 0.0), axis=(1, 3))
        square_sum, product_sum = jnp.sum(share(sums, ("section", "phase"), (S, Q), 0), axis=0)
        row_pos = (
            jnp.arange(blocks, dtype=jnp.int32)[None, :, None] * rows
            + ((k * 2 + jnp.arange(2, dtype=jnp.int32)[:, None, None]) * T + t) * sub
            + jnp.arange(sub, dtype=jnp.int32)[None, None, :]
        )
        target, old = returns_at(row_pos.reshape(-1), behavior, frozen, old_values, judge_ratings, lengths)
        target, old = target.reshape(square_sum.shape), old.reshape(square_sum.shape)
        rinv = lax.rsqrt(square_sum / D + EPSILON)
        values = rinv * product_sum
        squash = jnp.tanh((values - old) / CLIP_RANGE)
        clipped = old + CLIP_RANGE * squash
        loss_sum += 0.25 * jnp.sum((values - target) ** 2 + (clipped - target) ** 2)
        dvalue = 0.5 * (values - target) + 0.5 * (clipped - target) * (1.0 - squash * squash)
        rowwise = jnp.stack([rinv, dvalue, values / D])
        rowwise = jnp.sum(
            jnp.where(place[None, ..., None], rowwise[:, None, :, None], 0.0), axis=4
        )[..., None]
        normed = x * rowwise[0]
        head_sum += jnp.sum(normed * rowwise[1], axis=(0, 1, 2, 3))
        g = (rowwise[1] * rowwise[0] * (scale - normed * rowwise[2])).astype(BF16)
        local = g
        g = gather_tp(g.reshape(4 * nb, sub, C)).reshape(2, -1, C)
        grads[k] = [g[0], g[1]]

    hidden_rows = []
    sent = None
    for k in range(K):
        far, near = grads[k][1], grads[k][0]
        if k > 0:
            far, near = after(far, total), after(near, sent)
        far, near = (
            jnp.dot(g, turned, preferred_element_type=F32).reshape(2, nb, piece, FF) for g in (far, near)
        )
        total = near + xchg(far.astype(BF16), "section", 1).astype(F32)
        for h in range(2):
            x = total[h]
            for axis, mask in reversed(orders[h]):
                half = x.shape[0] // 2
                x = x[:half] + xchg(x[half:].astype(BF16), axis, mask).astype(F32)
                if half > 1:
                    sent = x
            hidden_rows.append(x.reshape(piece, FF).astype(BF16))
    hidden_grad = jnp.concatenate(hidden_rows, axis=0)

    all_hidden = jnp.concatenate([pieces[k][c].reshape(-1, FF) for k in range(K) for c in range(2)])
    all_grads = jnp.concatenate([grads[k][c] for k in range(K) for c in range(2)])
    all_grads = after(all_grads, total)
    down_projection_gradient = lax.dot_general(
        all_hidden, all_grads, (((0,), (0,)), ((), ())), preferred_element_type=F32
    )

    packed = after(jnp.concatenate([head_sum, loss_sum[None]]), total)
    packed = share(packed, ("section", "tp"), (S, T), 1).reshape(S, T, -1)
    packed = jnp.sum(packed, axis=1)
    total_loss, head_all = packed[0, -1], packed[:, :-1].reshape(-1)
    return (total_loss, gain * head_all, down_projection_gradient, hidden_grad)


def solution(mesh):
    shape = dict(mesh.shape)
    in_specs = (
        P(("section", "phase"), "tp"),
        P("tp", ("phase", "section")),
        P("section", "phase"),
        P("phase"),
        P("phase"),
        P(),
        P(),
        P(),
        P(),
        P(),
    )
    out_specs = (P(), P("phase"), P("tp", ("phase", "section")), P(("section", "phase"), "tp"))

    def run(*args):
        return on_device(shape, *args)

    return jax.shard_map(run, mesh=mesh, in_specs=in_specs, out_specs=out_specs, check_vma=False)
```

```python
import functools

import jax
import jax.numpy as jnp
from jax import lax
from jax.experimental import pallas as pl
from jax.experimental.layout import Layout, with_layout_constraint
from jax.experimental.pallas import tpu as pltpu
from jax.sharding import PartitionSpec as P

D = 8192

KL_PENALTY_SCALE = 0.1
TRACE_DECAY = 0.95
CLIP_RANGE = 0.2
EPSILON = 1e-05
BF16 = jnp.bfloat16
F32 = jnp.float32


def returns_at(row_pos, behavior, frozen, old_values, judge_ratings, lengths):
    total = behavior.shape[0]
    position = jnp.arange(total, dtype=jnp.int32)
    ends = jnp.cumsum(lengths)
    closes = position[:, None] == ends[None, :] - 1
    final = jnp.any(closes, axis=1)
    extra = jnp.sum(jnp.where(closes, judge_ratings[None, :], 0.0), axis=1)
    payoff = extra - KL_PENALTY_SCALE * (behavior - frozen)
    following = jnp.concatenate([old_values[1:], jnp.zeros_like(old_values[:1])])
    following = jnp.where(final, 0.0, following)
    delta = payoff + following - old_values
    segment = jnp.sum((position[:, None] >= ends[None, :]).astype(jnp.int32), axis=1)
    row_seg = jnp.sum((row_pos[:, None] >= ends[None, :]).astype(jnp.int32), axis=1)
    gap = position[None, :] - row_pos[:, None]
    inside = (row_seg[:, None] == segment[None, :]) & (gap >= 0)
    powers = jnp.power(F32(TRACE_DECAY), jnp.maximum(gap, 0).astype(F32))
    advantage = jnp.sum(jnp.where(inside, powers, 0.0) * delta[None, :], axis=1)
    own_old = jnp.sum(jnp.where(gap == 0, old_values[None, :], 0.0), axis=1)
    return advantage + own_old, own_old


def exchange_kernel(axes, sizes, x_ref, out_ref, slots, send_sems, recv_sems):
    n0, n1 = sizes
    n = n0 * n1
    a, b = lax.axis_index(axes[0]), lax.axis_index(axes[1])
    me = a * n1 + b

    def partner(i):
        return {axes[0]: lax.rem(a + i // n1, n0), axes[1]: lax.rem(b + i % n1, n1)}

    barrier = pltpu.get_barrier_semaphore()
    for i in range(1, n):
        pl.semaphore_signal(barrier, inc=1, device_id=partner(i), device_id_type=pl.DeviceIdType.MESH)
    pl.semaphore_wait(barrier, n - 1)
    copies = []
    for i in range(1, n):
        copy = pltpu.make_async_remote_copy(
            src_ref=x_ref, dst_ref=slots.at[me], send_sem=send_sems.at[i], recv_sem=recv_sems.at[i],
            device_id=partner(i), device_id_type=pl.DeviceIdType.MESH,
        )
        copy.start()
        copies.append(copy)
    slots[me] = x_ref[...]
    for copy in copies:
        copy.wait()
    out_ref[...] = slots[...]


def share(x, axes, sizes, collective_id):
    count = x.size
    tiles = -(-count // 1024) * 8
    flat = jnp.pad(x.reshape(-1), (0, tiles * 128 - count)).reshape(tiles, 128)
    n = sizes[0] * sizes[1]
    out = pl.pallas_call(
        functools.partial(exchange_kernel, axes, sizes),
        out_shape=jax.ShapeDtypeStruct((n, tiles, 128), F32),
        in_specs=[pl.BlockSpec(memory_space=pltpu.VMEM)],
        out_specs=pl.BlockSpec(memory_space=pltpu.VMEM),
        scratch_shapes=[
            pltpu.VMEM((n, tiles, 128), F32),
            pltpu.SemaphoreType.DMA((n,)),
            pltpu.SemaphoreType.DMA((n,)),
        ],
        compiler_params=pltpu.CompilerParams(collective_id=collective_id, has_side_effects=True),
    )(flat)
    return out.reshape(n, -1)[:, :count].reshape((n,) + x.shape)


def on_device(mesh_shape, hidden_act, down_weight, residual, head_weight, gain,
              behavior, frozen, old_values, judge_ratings, lengths):
    S, Q, T = mesh_shape["section"], mesh_shape["phase"], mesh_shape["tp"]
    s, p, t = (lax.axis_index(a) for a in ("section", "phase", "tp"))
    rows, FF = hidden_act.shape
    C = down_weight.shape[1]
    K = 2 if rows % (4 * T) == 0 else 1
    piece = rows // (2 * K)
    sub = piece // T
    sizes = {"section": S, "phase": Q, "tp": T}

    def xchg(x, axis, mask):
        return lax.ppermute(x, axis, [(i, i ^ mask) for i in range(sizes[axis])])

    phase_steps = [("phase", 1 << i) for i in range(Q.bit_length() - 1)]
    section_steps = [("section", 1 << i) for i in range(1, S.bit_length() - 1)]
    orders = [phase_steps + section_steps, section_steps + phase_steps]
    held = []
    for steps in orders:
        rs = [0]
        for axis, mask in steps:
            bit = mask * Q if axis == "section" else mask
            rs = rs + [r ^ bit for r in rs]
        held.append(rs)
    nb = len(held[0])
    me = s * Q + p
    own = hidden_act.reshape(K, 2, 1, piece, FF)

    def after(x, *others):
        for y in others:
            x = x + (0 * y[(0,) * y.ndim]).astype(x.dtype)
        return x

    def residual_parts(token):
        res = after(residual, token).reshape(Q, K, 2, T, sub, S, C)
        res = lax.dynamic_index_in_dim(res, t, 3, keepdims=False)
        for i in range(Q.bit_length() - 1):
            pairs = res.reshape((Q >> (i + 1), 2, 1 << i) + res.shape[1:])
            pairs = jnp.where((p >> i) & 1 == 1, pairs[:, ::-1], pairs)
            res = pairs.reshape(res.shape)
        res_by = []
        for m in range(S):
            part = lax.dynamic_index_in_dim(res, s ^ m, 4, keepdims=False)
            res_by.append(part if m == 0 else xchg(part, "section", m))
        return jnp.stack(res_by).reshape(S // 2, 2, Q, K, 2, sub, C)

    def reduce_tp(x):
        n, bit = T, 1
        while n > 1:
            y = x.reshape(x.shape[0], n // 2, 2, sub, C)
            up = (t & bit) != 0
            send = jnp.where(up, y[:, :, 0], y[:, :, 1]).astype(BF16)
            keep = jnp.where(up, y[:, :, 1], y[:, :, 0])
            x = keep + xchg(send, "tp", bit).astype(F32)
            n, bit = n // 2, bit * 2
        return x.reshape(-1, sub, C)

    def gather_tp(x):
        x = x[:, None]
        bit = T // 2
        while bit >= 1:
            got = xchg(x, "tp", bit)
            up = (t & bit) != 0
            lo, hi = jnp.where(up, got, x), jnp.where(up, x, got)
            x = jnp.stack([lo, hi], axis=2).reshape(x.shape[0], -1, sub, C)
            bit //= 2
        return x

    scale = lax.dynamic_slice_in_dim(gain * head_weight, s * C, C, 0)
    pieces = [None] * K
    combined = [None] * K
    products = [None] * K
    second, third = [], []
    for k in range(K):
        cur = [own[k, h] for h in range(2)]
        for j in range(len(orders[0])):
            got = [xchg(cur[h], *orders[h][j]) for h in range(2)]
            cur = [jnp.concatenate([cur[h], got[h]], axis=0) for h in range(2)]
            if j == 0:
                if k == 0:
                    turned = with_layout_constraint(down_weight.T, Layout((0, 1)))
                cur = [after(x, *second) for x in cur]
        here = after(jnp.stack(cur), *third)
        pieces[k] = [here, xchg(here, "section", 1)]
        if k == 0:
            res_by = residual_parts(got[0])
        outs = [
            jnp.dot(pieces[k][c].reshape(-1, FF), down_weight, preferred_element_type=F32)
            .reshape(2 * nb, T, sub, C)
            for c in range(2)
        ]
        base = jnp.stack([
            jnp.transpose(res_by[:, :, :, k, 0], (1, 0, 2, 3, 4)).reshape(2, nb, sub, C),
            jnp.transpose(res_by[:, :, :, k, 1], (1, 2, 0, 3, 4)).reshape(2, nb, sub, C),
        ], axis=1).reshape(4 * nb, sub, C)
        combined[k] = (base, outs)
        products[k] = outs
        second = [got[0], got[1], outs[0], jnp.max(turned[:16, :128], axis=0)]
        if k == 0:
            out = reduce_tp(jnp.concatenate(outs))
            combined[k] = combined[k][0].astype(F32) + out
            third = [combined[k]]

    blocks = S * Q
    rel = jnp.array([[r ^ (c * Q) for r in held[h]] for c in range(2) for h in range(2)], jnp.int32)
    place = (rel ^ me)[..., None] == jnp.arange(blocks, dtype=jnp.int32)
    place = place.reshape(2, 2, nb, blocks)
    loss_sum = F32(0)
    head_sum = jnp.zeros((C,), F32)
    grads = [[None, None] for _ in range(K)]
    for k in range(K):
        if k > 0:
            base, outs = combined[k]
            out = reduce_tp(jnp.concatenate(outs))
            combined[k] = after(base.astype(F32) + out, grads[k - 1][0])
        x = combined[k].reshape(2, 2, nb, sub, C)
        sums = jnp.stack([jnp.sum(x * x, axis=-1), jnp.sum(x * scale, axis=-1)])
        sums = jnp.sum(jnp.where(place[None, ..., None], sums[:, :, :, :, None, :], 0.0), axis=(1, 3))
        square_sum, product_sum = jnp.sum(share(sums, ("section", "phase"), (S, Q), 0), axis=0)
        row_pos = (
            jnp.arange(blocks, dtype=jnp.int32)[None, :, None] * rows
            + ((k * 2 + jnp.arange(2, dtype=jnp.int32)[:, None, None]) * T + t) * sub
            + jnp.arange(sub, dtype=jnp.int32)[None, None, :]
        )
        target, old = returns_at(row_pos.reshape(-1), behavior, frozen, old_values, judge_ratings, lengths)
        target, old = target.reshape(square_sum.shape), old.reshape(square_sum.shape)
        rinv = lax.rsqrt(square_sum / D + EPSILON)
        values = rinv * product_sum
        squash = jnp.tanh((values - old) / CLIP_RANGE)
        clipped = old + CLIP_RANGE * squash
        loss_sum += 0.25 * jnp.sum((values - target) ** 2 + (clipped - target) ** 2)
        dvalue = 0.5 * (values - target) + 0.5 * (clipped - target) * (1.0 - squash * squash)
        rowwise = jnp.stack([rinv, dvalue, values / D])
        rowwise = jnp.sum(
            jnp.where(place[None, ..., None], rowwise[:, None, :, None], 0.0), axis=4
        )[..., None]
        normed = x * rowwise[0]
        head_sum += jnp.sum(normed * rowwise[1], axis=(0, 1, 2, 3))
        g = (rowwise[1] * rowwise[0] * (scale - normed * rowwise[2])).astype(BF16)
        g = gather_tp(g.reshape(4 * nb, sub, C)).reshape(2, -1, C)
        grads[k] = [g[0], g[1]]

    hidden_rows = []
    sent = None
    for k in range(K):
        far, near = grads[k][1], grads[k][0]
        if k + 1 < K:
            far = after(far, products[k + 1][1])
        if k > 0:
            far, near = after(far, total), after(near, sent)
        far, near = (
            jnp.dot(g, turned, preferred_element_type=F32).reshape(2, nb, piece, FF) for g in (far, near)
        )
        total = near + xchg(far.astype(BF16), "section", 1).astype(F32)
        for h in range(2):
            x = total[h]
            for axis, mask in reversed(orders[h]):
                half = x.shape[0] // 2
                x = x[:half] + xchg(x[half:].astype(BF16), axis, mask).astype(F32)
                if half > 1:
                    sent = x
            hidden_rows.append(x.reshape(piece, FF).astype(BF16))
    hidden_grad = jnp.concatenate(hidden_rows, axis=0)

    all_hidden = jnp.concatenate([pieces[k][c].reshape(-1, FF) for k in range(K) for c in range(2)])
    all_grads = jnp.concatenate([grads[k][c] for k in range(K) for c in range(2)])
    all_grads = after(all_grads, total)
    down_projection_gradient = lax.dot_general(
        all_hidden, all_grads, (((0,), (0,)), ((), ())), preferred_element_type=F32
    )

    packed = after(jnp.concatenate([head_sum, loss_sum[None]]), total)
    packed = share(packed, ("section", "tp"), (S, T), 1).reshape(S, T, -1)
    packed = jnp.sum(packed, axis=1)
    total_loss, head_all = packed[0, -1], packed[:, :-1].reshape(-1)
    return (total_loss, gain * head_all, down_projection_gradient, hidden_grad)


def solution(mesh):
    shape = dict(mesh.shape)
    in_specs = (
        P(("section", "phase"), "tp"),
        P("tp", ("phase", "section")),
        P("section", "phase"),
        P("phase"),
        P("phase"),
        P(),
        P(),
        P(),
        P(),
        P(),
    )
    out_specs = (P(), P("phase"), P("tp", ("phase", "section")), P(("section", "phase"), "tp"))

    def run(*args):
        return on_device(shape, *args)

    return jax.shard_map(run, mesh=mesh, in_specs=in_specs, out_specs=out_specs, check_vma=False)
```
